256 devices in a mesh: dp: 16 (over x_hi, z), row: 8 (over y, core), col: 2 (over x_lo).
Axes of the slice: x: 4 (x_hi: 2, x_lo: 2; x = x_hi * 2 + x_lo), y: 4, z: 8, core: 2. Of those that a mesh axis runs over, the one named last changes fastest.
Arguments:
- activations: bfloat16 [2, 16384, 18432], P(None, 'dp', 'row'), may hold values from -6 to 6
- cotangent: bfloat16 [2, 16384, 1024], P(None, 'dp', 'col'), may hold values from -0.099436891 to 0.099436891
- weights: float32 [18432, 1024], P(('row', 'dp'), 'col'), may hold values from -6 to 6
- row_state: float32 [18432], P(('row', 'dp')), may hold values from 0.3 to 5.4
- col_state: float32 [1024], P('col'), may hold values from 0.05 to 8
Outputs:
- new_weights: float32 [18432, 1024], P(('row', 'dp'), 'col')
- compute_weights: bfloat16 [18432, 1024], P('row', 'col')
- new_row_state: float32 [18432], P(('row', 'dp'))
- new_col_state: float32 [1024], P('col')
The draws below stay inside these ranges and needn't reach their ends.
All inputs are finite; a program needn't handle non-finite values.
Results may differ from the reference program's by a relative error of at most 0.0004.
Values may be sent and summed in bfloat16 or wider, within the bound.
No kernel may reach another device: no remote copies, remote signals or barrier semaphores. Data moves between devices by JAX's collectives and lax.ppermute only.
A program may use at most 64 MiB of HBM per device.

```python
import math
import jax
import jax.numpy as jnp
from jax import lax

D = 18432
ROUNDS = 2
TOKENS = 16384
COLS = 1024
N_ROW = 8


def draw_row_state(key, part):
    key = jax.random.fold_in(key, 7)
    block_rows = D // N_ROW
    position = (jnp.arange(D, dtype=jnp.int32) % block_rows).astype(jnp.float32) / block_rows
    growth = jnp.exp(math.log(9.0) * position)
    factor = jnp.exp(jax.random.uniform(key, (D,), jnp.float32, math.log(0.3), math.log(0.6)))
    return factor * growth


def draw_col_state(key, part):
    key = jax.random.fold_in(key, 11)
    lower, upper = (0.05, 0.2)
    return jnp.exp(jax.random.uniform(key, (COLS,), jnp.float32, math.log(lower), math.log(upper)))


def draw_cotangent(key, part):
    key = jax.random.fold_in(key, 13)
    scale_key, value_key = jax.random.split(key)
    position = jnp.arange(COLS, dtype=jnp.int32).astype(jnp.float32) / COLS - 0.5
    base = 1.0 / math.sqrt(ROUNDS * TOKENS)
    rising = jnp.exp(math.log(6.0) * position)
    factor = jax.random.uniform(scale_key, (COLS,), jnp.float32, 0.7, 1.4)
    values = jnp.clip(jax.random.normal(value_key, (ROUNDS, TOKENS, COLS), jnp.float32), -4.0, 4.0)
    return (values * (base * rising * factor)[None, None, :]).astype(jnp.bfloat16)


def raised(array, stream_key, source, target, blocks, factor):
    owner, partner = [(jnp.arange(array.shape[dim]) // (array.shape[dim] // blocks)).reshape([-1 if axis == dim else 1 for axis in range(array.ndim)]) for dim in (source, target)]
    chosen = jax.random.permutation(stream_key, blocks)[partner]
    strong = (owner == chosen) | (owner == (partner + blocks // 2) % blocks)
    return jnp.where(strong, factor * array, array)


def levels(stream_key, shape, cuts, low, top_value):
    def one(dim, blocks):
        draws = jax.random.uniform(jax.random.fold_in(jax.random.fold_in(stream_key, 6), dim), (blocks,), jnp.float32, low / len(cuts), top_value / len(cuts))
        return jnp.repeat(jnp.exp(draws), shape[dim] // blocks).reshape((-1,) + (1,) * (len(shape) - dim - 1))

    gain = one(*cuts[0])
    for cut in cuts[1:]:
        gain = gain * one(*cut)
    return gain


def gaussian(key, extent, scale, bound, cuts=(), held_as=jnp.bfloat16):
    gain = levels(key, extent, cuts, -0.22, 0.18) if cuts else 1.0
    entries = jax.random.normal(key, extent, jnp.float32) * scale * gain
    return jnp.minimum(jnp.maximum(entries, -bound), bound).astype(held_as)


def bell_draw_with(rng, shape, width, limit, pieces, heavy, kind=jnp.bfloat16):
    values = width * jax.random.normal(rng, shape, jnp.float32)
    if pieces:
        values = values * levels(rng, shape, pieces, -0.22, 0.18)
    return jnp.clip(raised(values, jax.random.fold_in(rng, 3), *heavy), -limit, limit).astype(kind)


def setup_inputs(seed: int = 0) -> dict:
    key_list = jax.random.split(jax.random.key(seed), 6)
    activations = bell_draw_with(key_list[0], (ROUNDS, TOKENS, D), 1.0, 6.0, ((1, 16), (2, 8)), (1, 2, 16, 2.0))
    cotangent = draw_cotangent(jax.random.fold_in(key_list[5], 71), 0)
    weights = gaussian(key_list[2], (D, COLS), 1.0, 6.0, ((0, 128), (1, 2)), jnp.float32)
    row_state = draw_row_state(jax.random.fold_in(key_list[5], 71), 0)
    col_state = draw_col_state(jax.random.fold_in(key_list[5], 71), 0)
    return dict(activations=activations, cotangent=cotangent, weights=weights, row_state=row_state, col_state=col_state)


beta_two = 0.8
epsilon_one = 1e-30
step_size = 0.05

def reference(activations, cotangent, weights, row_state, col_state):
    gradient = jnp.zeros((D, COLS), jnp.float32)
    for round_index in range(ROUNDS):
        gradient = gradient + jnp.dot(activations[round_index].T, cotangent[round_index], preferred_element_type=jnp.float32)
    squares = gradient * gradient
    new_row_state = beta_two * row_state + (1.0 - beta_two) * (lax.optimization_barrier(jnp.mean(squares, axis=1)) + epsilon_one)
    new_col_state = beta_two * col_state + (1.0 - beta_two) * (lax.optimization_barrier(jnp.mean(squares, axis=0)) + epsilon_one)
    row_mean = jnp.mean(new_row_state)
    scaled = gradient * lax.rsqrt(new_row_state[:, None] * new_col_state[None, :] / row_mean)
    update_rms = jnp.sqrt(jnp.mean(scaled * scaled))
    update = scaled / jnp.maximum(1.0, update_rms)
    new_weights = weights - step_size * update
    return (new_weights, new_weights.astype(jnp.bfloat16), new_row_state, new_col_state)
```

```python
import jax
import jax.numpy as jnp
from jax import lax
from jax.sharding import PartitionSpec as P

beta_two = 0.8
epsilon_one = 1e-30
step_size = 0.05

X_HALVES = 2
SEND_SCALE = 4.0
RS_PARTS = 2
AG_PARTS = 2


def around_z(n_z, hop):
    return [(x * n_z + z, x * n_z + (z + hop) % n_z) for x in range(X_HALVES) for z in range(n_z)]


def across_x(n_z):
    return [(x * n_z + z, (1 - x) * n_z + z) for x in range(X_HALVES) for z in range(n_z)]


def shards(activations, cotangent, weights, row_state, col_state):
    f32 = jnp.float32
    n_dp = lax.axis_size("dp")
    n_row = lax.axis_size("row")
    n_z = n_dp // X_HALVES
    rows, columns = weights.shape
    rows_all = rows * n_dp * n_row
    columns_all = columns * lax.axis_size("col")
    place = lax.axis_index("dp")
    z = lax.rem(place, n_z)
    x_half = lax.div(place, n_z)
    up, down, swap = around_z(n_z, 1), around_z(n_z, -1), across_x(n_z)
    half = rows

    def block(array, offset):
        return lax.dynamic_index_in_dim(array, lax.rem(z + offset + n_z, n_z), 1, keepdims=False)

    with jax.named_scope("partner_shard"):
        other_weights = lax.ppermute(weights, "dp", swap)
        other_state = lax.ppermute(row_state, "dp", swap)
        first = x_half == 0
        pair_weights = jnp.where(
            first, jnp.stack([weights, other_weights]), jnp.stack([other_weights, weights])
        )
        pair_state = jnp.where(
            first, jnp.stack([row_state, other_state]), jnp.stack([other_state, row_state])
        )

    def partial(part, parts):
        width = columns // parts
        outer = lax.slice_in_dim(cotangent, part * width, (part + 1) * width, axis=2)
        product = lax.dot_general(
            activations, outer, (((0, 1), (0, 1)), ((), ())), preferred_element_type=f32
        )
        return (product * SEND_SCALE).astype(jnp.float16).reshape(X_HALVES, n_z, rows, width)

    with jax.named_scope("gradient"):
        sums = [partial(p, RS_PARTS) for p in range(RS_PARTS)]

    def send_both(pairs):
        return [
            (lax.ppermute(a, "dp", up), lax.ppermute(b, "dp", down)) for a, b in pairs
        ]

    with jax.named_scope("reduce_ring"):
        far = n_z // 2
        held = []
        for s in sums:
            b = block(s, far)
            held.append((b[0], b[1]))
        held = send_both(held)
        for hop in range(far - 1, 0, -1):
            nxt = []
            for s, (a, b) in zip(sums, held):
                mine_up = block(s, hop).astype(f32)
                mine_down = block(s, -hop).astype(f32)
                if hop == far - 1:
                    mine_up = jnp.stack([mine_up[0] + a.astype(f32), mine_up[1]])
                    mine_down = jnp.stack([mine_down[0], mine_down[1] + b.astype(f32)])
                else:
                    mine_up = mine_up + a.astype(f32)
                    mine_down = mine_down + b.astype(f32)
                nxt.append((mine_up.astype(jnp.float16), mine_down.astype(jnp.float16)))
            held = send_both(nxt)
        mine = [
            (block(s, 0).astype(f32) + a.astype(f32) + b.astype(f32)).astype(jnp.float16)
            for s, (a, b) in zip(sums, held)
        ]
    with jax.named_scope("reduce_pair"):
        theirs = [lax.ppermute(m, "dp", swap) for m in mine]
        gradient = jnp.concatenate(
            [
                (m.astype(f32) + t.astype(f32)) * (1.0 / SEND_SCALE)
                for m, t in zip(mine, theirs)
            ],
            axis=2,
        )
    with jax.named_scope("statistics"):
        squares = gradient * gradient
        local_rows = jnp.sum(squares, axis=2)
        row_total = local_rows + lax.ppermute(local_rows, "col", [(0, 1), (1, 0)])
        new_rows = beta_two * pair_state + (1.0 - beta_two) * (
            row_total / columns_all + epsilon_one
        )
        local_cols = jnp.sum(squares, axis=(0, 1))
        weighed_cols = jnp.sum(squares / new_rows[:, :, None], axis=(0, 1))
        state_sum = jnp.sum(new_rows)
        lanes = 128
        vector = jnp.concatenate([local_cols, weighed_cols, jnp.full((lanes,), state_sum, f32)])
        vector = vector.reshape(-1, lanes)

        def total(v, axis, size, groups):
            copies = jnp.broadcast_to(v[None], (size,) + v.shape)
            got = lax.all_to_all(copies, axis, 0, 0, axis_index_groups=groups)
            return jnp.sum(got, axis=0)

        vector = total(
            vector, "dp", n_z, [[x * n_z + i for i in range(n_z)] for x in range(X_HALVES)]
        )
        vector = total(vector, "row", n_row, None)
        flat = vector.reshape(-1)
        col_total, weighed_total = flat[:columns], flat[columns : 2 * columns]
        row_mean = flat[2 * columns] / rows_all
        new_cols = beta_two * col_state + (1.0 - beta_two) * (col_total / rows_all + epsilon_one)
        part_square = jnp.sum(weighed_total / new_cols).reshape(1, 1)
        square_total = part_square + lax.ppermute(part_square, "col", [(0, 1), (1, 0)])
        update_rms = jnp.sqrt(square_total[0, 0] * row_mean / (rows_all * columns_all))
    with jax.named_scope("update"):
        rate = step_size / jnp.maximum(1.0, update_rms)
        row_factor = lax.rsqrt(new_rows / row_mean) * rate
        pair_new = pair_weights - gradient * row_factor[:, :, None] * lax.rsqrt(new_cols)
        new_weights = lax.dynamic_index_in_dim(pair_new, x_half, 0, keepdims=False)
        new_row_state = lax.dynamic_index_in_dim(new_rows, x_half, 0, keepdims=False)
        rounded = pair_new.astype(jnp.bfloat16)
    with jax.named_scope("gather_ring"):
        width = columns // AG_PARTS
        gathered = jnp.zeros((X_HALVES, n_z, rows, columns), jnp.bfloat16)

        def put(array, value, offset, part, x_start=0):
            start = (x_start, lax.rem(z + offset + n_z, n_z), 0, part * width)
            return lax.dynamic_update_slice(array, value[:, None], start)

        gathered = lax.dynamic_update_slice(gathered, rounded[:, None], (0, z, 0, 0))
        held = []
        for p in range(AG_PARTS):
            own = rounded[:, :, p * width : (p + 1) * width]
            held.append((own, own))
        for hop in range(1, far):
            held = send_both(held)
            for p, (a, b) in enumerate(held):
                gathered = put(gathered, a, -hop, p)
                gathered = put(gathered, b, hop, p)
        held = send_both([(a[:1], b[1:]) for a, b in held])
        for p, (a, b) in enumerate(held):
            gathered = put(gathered, a, far, p, 0)
            gathered = put(gathered, b, far, p, 1)
        compute_weights = gathered.reshape(n_dp * rows, columns)
    return (new_weights, compute_weights, new_row_state, new_cols)


def solution(mesh):
    placed = (
        P(None, "dp", "row"),
        P(None, "dp", "col"),
        P(("row", "dp"), "col"),
        P(("row", "dp")),
        P("col"),
    )
    return jax.shard_map(
        shards,
        mesh=mesh,
        in_specs=placed,
        out_specs=(P(("row", "dp"), "col"), P("row", "col"), P(("row", "dp")), P("col")),
        check_vma=False,
    )
```

```python
import jax
import jax.numpy as jnp
from jax import lax
from jax.sharding import PartitionSpec as P

beta_two = 0.8
epsilon_one = 1e-30
step_size = 0.05

X_HALVES = 2
SEND_SCALE = 4.0
PARTS = 2


def around_z(n_z, n_row, hop):
    pairs = []
    for x in range(X_HALVES):
        for z in range(n_z):
            for row in range(n_row):
                there = (z + (hop if row % 2 == 0 else -hop)) % n_z
                pairs.append(((x * n_z + z) * n_row + row, (x * n_z + there) * n_row + row))
    return pairs


def across_x(n_z):
    return [(x * n_z + z, (1 - x) * n_z + z) for x in range(X_HALVES) for z in range(n_z)]


def shards(activations, cotangent, weights, row_state, col_state):
    f32, f16 = jnp.float32, jnp.float16
    lanes = 128
    n_dp = lax.axis_size("dp")
    n_row = lax.axis_size("row")
    n_z = n_dp // X_HALVES
    far = n_z // 2
    rows, columns = weights.shape
    rows_all = rows * n_dp * n_row
    columns_all = columns * lax.axis_size("col")
    place = lax.axis_index("dp")
    z = lax.rem(place, n_z)
    first = lax.div(place, n_z) == 0
    way = 1 - 2 * lax.rem(lax.axis_index("row"), 2)
    up, down = around_z(n_z, n_row, 1), around_z(n_z, n_row, -1)
    swap = across_x(n_z)
    ones = jnp.ones((lanes, lanes), f32)

    def spread_sum(array):
        return lax.dot_general(
            jnp.sum(array.reshape(-1, lanes), axis=0, keepdims=True),
            ones,
            (((1,), (0,)), ((), ())),
            precision=lax.Precision.HIGHEST,
            preferred_element_type=f32,
        )

    def ordered(own, other):
        return [jnp.where(first, own, other), jnp.where(first, other, own)]

    def beside(offset):
        return lax.rem(z + way * offset + n_z, n_z)

    def block(array, offset):
        return lax.dynamic_index_in_dim(array, beside(offset), 1, keepdims=False)

    def send_both(pairs):
        both = ("dp", "row")
        return [(lax.ppermute(a, both, up), lax.ppermute(b, both, down)) for a, b in pairs]

    with jax.named_scope("partner_weights"):
        other_weights = lax.ppermute(weights, "dp", swap)

    with jax.named_scope("gradient"):
        width = columns // PARTS
        sums = []
        for part in range(PARTS):
            product = lax.dot_general(
                activations,
                lax.slice_in_dim(cotangent, part * width, (part + 1) * width, axis=2),
                (((0, 1), (0, 1)), ((), ())),
                preferred_element_type=f32,
            )
            sums.append((product * SEND_SCALE).astype(f16).reshape(X_HALVES, n_z, rows, width))

    with jax.named_scope("reduce_ring"):
        held = []
        for s in sums:
            b = block(s, far)
            held.append((b[0], b[1]))
        held = send_both(held)
        for hop in range(far - 1, 0, -1):
            sent = []
            for s, (a, b) in zip(sums, held):
                mine_up, mine_down = block(s, hop).astype(f32), block(s, -hop).astype(f32)
                a, b = a.astype(f32), b.astype(f32)
                if hop == far - 1:
                    mine_up = jnp.stack([mine_up[0] + a, mine_up[1]])
                    mine_down = jnp.stack([mine_down[0], mine_down[1] + b])
                else:
                    mine_up, mine_down = mine_up + a, mine_down + b
                sent.append((mine_up.astype(f16), mine_down.astype(f16)))
            held = send_both(sent)
        mine = [
            (block(s, 0).astype(f32) + a.astype(f32) + b.astype(f32)).astype(f16)
            for s, (a, b) in zip(sums, held)
        ]
    with jax.named_scope("reduce_pair"):
        theirs = [lax.ppermute(m, "dp", swap) for m in mine]
        both = jnp.concatenate(
            [
                (m.astype(f32) + t.astype(f32)) * (1.0 / SEND_SCALE)
                for m, t in zip(mine, theirs)
            ],
            axis=2,
        )
        gradient = [both[x] for x in range(X_HALVES)]
    with jax.named_scope("row_statistics"):
        local_rows = jnp.stack([jnp.sum(g * g, axis=1) for g in gradient])
        corner = [
            (2 * i + c, 2 * j + 1 - c) for i, j in across_x(n_z) for c in range(2)
        ]
        lines = columns // lanes
        tail = (0, max(rows, lanes) - rows)
        mail = [
            jnp.pad(local_rows, ((0, 0), tail)),
            jnp.pad(row_state[None], ((0, 0), tail)),
            jnp.pad(col_state.reshape(lines, lanes), ((0, 0), (0, max(rows, lanes) - lanes))),
        ]
        got = lax.ppermute(jnp.concatenate(mail), ("dp", "col"), corner)
        got_rows, got_state = got[:X_HALVES, :rows], got[X_HALVES, :rows]
        got_cols = got[X_HALVES + 1 :, :lanes]
        row_total = local_rows + got_rows
        pair_state = jnp.stack(ordered(row_state, got_state))
        new_rows = beta_two * pair_state + (1.0 - beta_two) * (
            row_total / columns_all + epsilon_one
        )
    with jax.named_scope("column_statistics"):
        inverse = 1.0 / new_rows
        local_cols = sum(jnp.sum(g * g, axis=0) for g in gradient)
        weighed_cols = sum(
            jnp.sum(g * g * inverse[x][:, None], axis=0) for x, g in enumerate(gradient)
        )
        pad = -(X_HALVES * rows) % lanes
        state_sum = spread_sum(jnp.pad(new_rows.reshape(-1), (0, pad)))
        vector = jnp.concatenate(
            [local_cols.reshape(-1, lanes), weighed_cols.reshape(-1, lanes), state_sum]
        )

        def spread(v, axis, size, groups=None):
            copies = jnp.broadcast_to(v[None], (size,) + v.shape)
            return lax.all_to_all(copies, axis, 0, 0, axis_index_groups=groups)

        z_groups = [[x * n_z + i for i in range(n_z)] for x in range(X_HALVES)]
        vector = jnp.sum(spread(vector, "dp", n_z, z_groups), axis=0)
        n_col = lax.axis_size("col")
        halves = spread(vector, ("row", "col"), n_row * n_col)
        halves = jnp.sum(halves.reshape(n_row, n_col, *vector.shape), axis=0)
        left = lax.axis_index("col") == 0
        own_cols = col_state.reshape(lines, lanes)
        states = jnp.stack(
            [jnp.where(left, own_cols, got_cols), jnp.where(left, got_cols, own_cols)]
        )
        both_cols = beta_two * states + (1.0 - beta_two) * (
            halves[:, :lines] / rows_all + epsilon_one
        )
        new_cols = jnp.where(left, both_cols[0], both_cols[1])
        row_mean = halves[0, 2 * lines :] / rows_all
        share = halves[:, lines : 2 * lines] / both_cols
        mean_square = spread_sum(share) * row_mean / (rows_all * columns_all)
    with jax.named_scope("update"):
        rate = step_size / jnp.maximum(1.0, jnp.sqrt(mean_square))
        col_factor = (lax.rsqrt(new_cols / row_mean) * rate).reshape(1, columns)
        row_factor = lax.rsqrt(new_rows)
        pair_weights = ordered(weights, other_weights)
        pair_new = [
            w - g * row_factor[x][:, None] * col_factor
            for x, (w, g) in enumerate(zip(pair_weights, gradient))
        ]
        new_weights = jnp.where(first, pair_new[0], pair_new[1])
        new_row_state = jnp.where(first, new_rows[0], new_rows[1])
        rounded = [w.astype(jnp.bfloat16) for w in pair_new]
    with jax.named_scope("gather_ring"):
        middle = columns // 2
        gathered = jnp.zeros((X_HALVES, n_z, rows, columns), jnp.bfloat16)

        def put(array, value, offset, x, column=0):
            start = (x, beside(offset), 0, column)
            return lax.dynamic_update_slice(array, value[None, None], start)

        for x, r in enumerate(rounded):
            gathered = put(gathered, r, 0, x)
        held = [(r, r) for r in rounded]
        for hop in range(1, far):
            held = send_both(held)
            for x, (a, b) in enumerate(held):
                gathered = put(gathered, a, -hop, x)
                gathered = put(gathered, b, hop, x)
        held = send_both([(a[:, :middle], b[:, middle:]) for a, b in held])
        for x, (a, b) in enumerate(held):
            gathered = put(gathered, a, far, x)
            gathered = put(gathered, b, far, x, middle)
        compute_weights = gathered.reshape(n_dp * rows, columns)
    return (new_weights, compute_weights, new_row_state, new_cols.reshape(columns))


def solution(mesh):
    placed = (
        P(None, "dp", "row"),
        P(None, "dp", "col"),
        P(("row", "dp"), "col"),
        P(("row", "dp")),
        P("col"),
    )
    return jax.shard_map(
        shards,
        mesh=mesh,
        in_specs=placed,
        out_specs=(P(("row", "dp"), "col"), P("row", "col"), P(("row", "dp")), P("col")),
        check_vma=False,
    )
```

```python
import jax
import jax.numpy as jnp
from jax import lax
from jax.sharding import PartitionSpec as P

beta_two = 0.8
epsilon_one = 1e-30
step_size = 0.05

X_HALVES = 2
SEND_SCALE = 4.0
PARTS = 2


def around_z(n_z, n_row, hop):
    pairs = []
    for x in range(X_HALVES):
        for z in range(n_z):
            for row in range(n_row):
                there = (z + (hop if row % 2 == 0 else -hop)) % n_z
                pairs.append(((x * n_z + z) * n_row + row, (x * n_z + there) * n_row + row))
    return pairs


def across_x(n_z):
    return [(x * n_z + z, (1 - x) * n_z + z) for x in range(X_HALVES) for z in range(n_z)]


def shards(activations, cotangent, weights, row_state, col_state):
    f32, f16 = jnp.float32, jnp.float16
    lanes = 128
    n_dp = lax.axis_size("dp")
    n_row = lax.axis_size("row")
    n_z = n_dp // X_HALVES
    far = n_z // 2
    rows, columns = weights.shape
    rows_all = rows * n_dp * n_row
    columns_all = columns * lax.axis_size("col")
    place = lax.axis_index("dp")
    z = lax.rem(place, n_z)
    first = lax.div(place, n_z) == 0
    way = 1 - 2 * lax.rem(lax.axis_index("row"), 2)
    swap = across_x(n_z)
    ones = jnp.ones((lanes, lanes), f32)

    def spread_sum(array):
        return lax.dot_general(
            jnp.sum(array.reshape(-1, lanes), axis=0, keepdims=True),
            ones,
            (((1,), (0,)), ((), ())),
            precision=lax.Precision.HIGHEST,
            preferred_element_type=f32,
        )

    def ordered(own, other):
        return [jnp.where(first, own, other), jnp.where(first, other, own)]

    def beside(offset):
        return lax.rem(z + way * offset + n_z, n_z)

    def block(array, offset):
        return lax.dynamic_index_in_dim(array, beside(offset), 1, keepdims=False)

    def send_both(pairs, hop=1):
        both = ("dp", "row")
        up, down = around_z(n_z, n_row, hop), around_z(n_z, n_row, -hop)
        return [(lax.ppermute(a, both, up), lax.ppermute(b, both, down)) for a, b in pairs]

    with jax.named_scope("partner_weights"):
        other_weights = lax.ppermute(weights, "dp", swap)

    with jax.named_scope("gradient"):
        width = columns // PARTS
        sums = []
        for part in range(PARTS):
            product = lax.dot_general(
                activations,
                lax.slice_in_dim(cotangent, part * width, (part + 1) * width, axis=2),
                (((0, 1), (0, 1)), ((), ())),
                preferred_element_type=f32,
            )
            sums.append((product * SEND_SCALE).astype(f16).reshape(X_HALVES, n_z, rows, width))

    with jax.named_scope("reduce_ring"):
        opening = send_both([(block(s, far - 1), block(s, 1 - far)) for s in sums])
        leap = [
            lax.ppermute(block(s, far), ("dp", "row"), around_z(n_z, n_row, hop))
            for s, hop in zip(sums, (2, -2))
        ]
        held = opening
        for hop in range(far - 2, 0, -1):
            sent = []
            for p, (s, (a, b)) in enumerate(zip(sums, held)):
                mine_up = block(s, hop).astype(f32) + a.astype(f32)
                mine_down = block(s, -hop).astype(f32) + b.astype(f32)
                if hop == far - 2 and p == 0:
                    mine_up = mine_up + leap[0].astype(f32)
                if hop == far - 2 and p == 1:
                    mine_down = mine_down + leap[1].astype(f32)
                sent.append((mine_up.astype(f16), mine_down.astype(f16)))
            held = send_both(sent)
        mine = [
            (block(s, 0).astype(f32) + a.astype(f32) + b.astype(f32)).astype(f16)
            for s, (a, b) in zip(sums, held)
        ]
    with jax.named_scope("reduce_pair"):
        theirs = [lax.ppermute(m, "dp", swap) for m in mine]
        both = jnp.concatenate(
            [
                (m.astype(f32) + t.astype(f32)) * (1.0 / SEND_SCALE)
                for m, t in zip(mine, theirs)
            ],
            axis=2,
        )
        gradient = [both[x] for x in range(X_HALVES)]
    with jax.named_scope("row_statistics"):
        local_rows = jnp.stack([jnp.sum(g * g, axis=1) for g in gradient])
        corner = [
            (2 * i + c, 2 * j + 1 - c) for i, j in across_x(n_z) for c in range(2)
        ]
        lines = columns // lanes
        tail = (0, max(rows, lanes) - rows)
        mail = [
            jnp.pad(local_rows, ((0, 0), tail)),
            jnp.pad(row_state[None], ((0, 0), tail)),
            jnp.pad(col_state.reshape(lines, lanes), ((0, 0), (0, max(rows, lanes) - lanes))),
        ]
        got = lax.ppermute(jnp.concatenate(mail), ("dp", "col"), corner)
        got_rows, got_state = got[:X_HALVES, :rows], got[X_HALVES, :rows]
        got_cols = got[X_HALVES + 1 :, :lanes]
        row_total = local_rows + got_rows
        pair_state = jnp.stack(ordered(row_state, got_state))
        new_rows = beta_two * pair_state + (1.0 - beta_two) * (
            row_total / columns_all + epsilon_one
        )
    with jax.named_scope("column_statistics"):
        inverse = 1.0 / new_rows
        local_cols = sum(jnp.sum(g * g, axis=0) for g in gradient)
        weighed_cols = sum(
            jnp.sum(g * g * inverse[x][:, None], axis=0) for x, g in enumerate(gradient)
        )
        pad = -(X_HALVES * rows) % lanes
        state_sum = spread_sum(jnp.pad(new_rows.reshape(-1), (0, pad)))
        vector = jnp.concatenate(
            [local_cols.reshape(-1, lanes), weighed_cols.reshape(-1, lanes), state_sum]
        )

        def spread(v, axis, size, groups=None):
            copies = jnp.broadcast_to(v[None], (size,) + v.shape)
            return lax.all_to_all(copies, axis, 0, 0, axis_index_groups=groups)

        z_groups = [[x * n_z + i for i in range(n_z)] for x in range(X_HALVES)]
        vector = jnp.sum(spread(vector, "dp", n_z, z_groups), axis=0)
        n_col = lax.axis_size("col")
        halves = spread(vector, ("row", "col"), n_row * n_col)
        halves = jnp.sum(halves.reshape(n_row, n_col, *vector.shape), axis=0)
        left = lax.axis_index("col") == 0
        own_cols = col_state.reshape(lines, lanes)
        states = jnp.stack(
            [jnp.where(left, own_cols, got_cols), jnp.where(left, got_cols, own_cols)]
        )
        both_cols = beta_two * states + (1.0 - beta_two) * (
            halves[:, :lines] / rows_all + epsilon_one
        )
        new_cols = jnp.where(left, both_cols[0], both_cols[1])
        row_mean = halves[0, 2 * lines :] / rows_all
        share = halves[:, lines : 2 * lines] / both_cols
        mean_square = spread_sum(share) * row_mean / (rows_all * columns_all)
    with jax.named_scope("update"):
        rate = step_size / jnp.maximum(1.0, jnp.sqrt(mean_square))
        col_factor = (lax.rsqrt(new_cols / row_mean) * rate).reshape(1, columns)
        row_factor = lax.rsqrt(new_rows)
        pair_weights = ordered(weights, other_weights)
        pair_new = [
            w - g * row_factor[x][:, None] * col_factor
            for x, (w, g) in enumerate(zip(pair_weights, gradient))
        ]
        new_weights = jnp.where(first, pair_new[0], pair_new[1])
        new_row_state = jnp.where(first, new_rows[0], new_rows[1])
        rounded = [w.astype(jnp.bfloat16) for w in pair_new]
    with jax.named_scope("gather_ring"):
        gathered = jnp.zeros((X_HALVES, n_z, rows, columns), jnp.bfloat16)

        def put(array, value, offset, x):
            start = (x, beside(offset), 0, 0)
            return lax.dynamic_update_slice(array, value[None, None], start)

        for x, r in enumerate(rounded):
            gathered = put(gathered, r, 0, x)
        held = [(r, r) for r in rounded]
        for hop in range(1, far):
            if hop == far - 1:
                last = [
                    lax.ppermute(held[x][x], ("dp", "row"), around_z(n_z, n_row, step))
                    for x, step in enumerate((2, -2))
                ]
            held = send_both(held)
            for x, (a, b) in enumerate(held):
                gathered = put(gathered, a, -hop, x)
                gathered = put(gathered, b, hop, x)
        for x, block_far in enumerate(last):
            gathered = put(gathered, block_far, far, x)
        compute_weights = gathered.reshape(n_dp * rows, columns)
    return (new_weights, compute_weights, new_row_state, new_cols.reshape(columns))


def solution(mesh):
    placed = (
        P(None, "dp", "row"),
        P(None, "dp", "col"),
        P(("row", "dp"), "col"),
        P(("row", "dp")),
        P("col"),
    )
    return jax.shard_map(
        shards,
        mesh=mesh,
        in_specs=placed,
        out_specs=(P(("row", "dp"), "col"), P("row", "col"), P(("row", "dp")), P("col")),
        check_vma=False,
    )
```

```python
import jax
import jax.numpy as jnp
from jax import lax
from jax.sharding import PartitionSpec as P

beta_two = 0.8
epsilon_one = 1e-30
step_size = 0.05

X_HALVES = 2
SEND_SCALE = 4.0
PARTS = 2


def around_z(n_z, n_row, hop):
    pairs = []
    for x in range(X_HALVES):
        for z in range(n_z):
            for row in range(n_row):
                there = (z + (hop if row % 2 == 0 else -hop)) % n_z
                pairs.append(((x * n_z + z) * n_row + row, (x * n_z + there) * n_row + row))
    return pairs


def across_x(n_z):
    return [(x * n_z + z, (1 - x) * n_z + z) for x in range(X_HALVES) for z in range(n_z)]


def shards(activations, cotangent, weights, row_state, col_state):
    f32, f16 = jnp.float32, jnp.float16
    lanes = 128
    n_dp = lax.axis_size("dp")
    n_row = lax.axis_size("row")
    n_z = n_dp // X_HALVES
    far = n_z // 2
    rows, columns = weights.shape
    rows_all = rows * n_dp * n_row
    columns_all = columns * lax.axis_size("col")
    place = lax.axis_index("dp")
    z = lax.rem(place, n_z)
    first = lax.div(place, n_z) == 0
    way = 1 - 2 * lax.rem(lax.axis_index("row"), 2)
    swap = across_x(n_z)
    ones = jnp.ones((lanes, lanes), f32)

    def spread_sum(array):
        return lax.dot_general(
            jnp.sum(array.reshape(-1, lanes), axis=0, keepdims=True),
            ones,
            (((1,), (0,)), ((), ())),
            precision=lax.Precision.HIGHEST,
            preferred_element_type=f32,
        )

    def ordered(own, other):
        return [jnp.where(first, own, other), jnp.where(first, other, own)]

    def beside(offset):
        return lax.rem(z + way * offset + n_z, n_z)

    def block(array, offset):
        return lax.dynamic_index_in_dim(array, beside(offset), 1, keepdims=False)

    def send_both(pairs, hop=1):
        both = ("dp", "row")
        up, down = around_z(n_z, n_row, hop), around_z(n_z, n_row, -hop)
        return [(lax.ppermute(a, both, up), lax.ppermute(b, both, down)) for a, b in pairs]

    with jax.named_scope("partner_weights"):
        other_weights = lax.ppermute(weights, "dp", swap)

    with jax.named_scope("gradient"):
        width = columns // PARTS
        sums = []
        for part in range(PARTS):
            product = lax.dot_general(
                activations,
                lax.slice_in_dim(cotangent, part * width, (part + 1) * width, axis=2),
                (((0, 1), (0, 1)), ((), ())),
                preferred_element_type=f32,
            )
            sums.append((product * SEND_SCALE).astype(f16).reshape(X_HALVES, n_z, rows, width))

    with jax.named_scope("reduce_ring"):
        leap = [
            lax.ppermute(block(s, far), ("dp", "row"), around_z(n_z, n_row, hop))
            for s, hop in zip(sums, (2, -2))
        ]
        held = send_both([(block(s, far - 1), block(s, 1 - far)) for s in sums])
        for hop in range(far - 2, 0, -1):
            sent = []
            for p, (s, (a, b)) in enumerate(zip(sums, held)):
                mine_up = block(s, hop).astype(f32) + a.astype(f32)
                mine_down = block(s, -hop).astype(f32) + b.astype(f32)
                if hop == far - 2 and p == 0:
                    mine_up = mine_up + leap[0].astype(f32)
                if hop == far - 2 and p == 1:
                    mine_down = mine_down + leap[1].astype(f32)
                sent.append((mine_up.astype(f16), mine_down.astype(f16)))
            held = send_both(sent)
        mine = [
            (block(s, 0).astype(f32) + a.astype(f32) + b.astype(f32)).astype(f16)
            for s, (a, b) in zip(sums, held)
        ]
    with jax.named_scope("reduce_pair"):
        theirs = [lax.ppermute(m, "dp", swap) for m in mine]
        both = jnp.concatenate(
            [
                (m.astype(f32) + t.astype(f32)) * (1.0 / SEND_SCALE)
                for m, t in zip(mine, theirs)
            ],
            axis=2,
        )
        gradient = [both[x] for x in range(X_HALVES)]
    with jax.named_scope("row_statistics"):
        local_rows = jnp.stack([jnp.sum(g * g, axis=1) for g in gradient])
        corner = [
            (2 * i + c, 2 * j + 1 - c) for i, j in across_x(n_z) for c in range(2)
        ]
        lines = columns // lanes
        tail = (0, max(rows, lanes) - rows)
        mail = [
            jnp.pad(local_rows, ((0, 0), tail)),
            jnp.pad(row_state[None], ((0, 0), tail)),
            jnp.pad(col_state.reshape(lines, lanes), ((0, 0), (0, max(rows, lanes) - lanes))),
        ]
        got = lax.ppermute(jnp.concatenate(mail), ("dp", "col"), corner)
        got_rows, got_state = got[:X_HALVES, :rows], got[X_HALVES, :rows]
        got_cols = got[X_HALVES + 1 :, :lanes]
        row_total = local_rows + got_rows
        pair_state = jnp.stack(ordered(row_state, got_state))
        new_rows = beta_two * pair_state + (1.0 - beta_two) * (
            row_total / columns_all + epsilon_one
        )
    with jax.named_scope("column_statistics"):
        inverse = 1.0 / new_rows
        local_cols = sum(jnp.sum(g * g, axis=0) for g in gradient)
        weighed_cols = sum(
            jnp.sum(g * g * inverse[x][:, None], axis=0) for x, g in enumerate(gradient)
        )
        pad = -(X_HALVES * rows) % lanes
        state_sum = spread_sum(jnp.pad(new_rows.reshape(-1), (0, pad)))
        vector = jnp.concatenate(
            [local_cols.reshape(-1, lanes), weighed_cols.reshape(-1, lanes), state_sum]
        )

        def spread(v, axis, size, groups=None):
            copies = jnp.broadcast_to(v[None], (size,) + v.shape)
            return lax.all_to_all(copies, axis, 0, 0, axis_index_groups=groups)

        z_groups = [[x * n_z + i for i in range(n_z)] for x in range(X_HALVES)]
        vector = jnp.sum(spread(vector, "dp", n_z, z_groups), axis=0)
        n_col = lax.axis_size("col")
        halves = spread(vector, ("row", "col"), n_row * n_col)
        halves = jnp.sum(halves.reshape(n_row, n_col, *vector.shape), axis=0)
        left = lax.axis_index("col") == 0
        own_cols = col_state.reshape(lines, lanes)
        states = jnp.stack(
            [jnp.where(left, own_cols, got_cols), jnp.where(left, got_cols, own_cols)]
        )
        both_cols = beta_two * states + (1.0 - beta_two) * (
            halves[:, :lines] / rows_all + epsilon_one
        )
        new_cols = jnp.where(left, both_cols[0], both_cols[1])
        row_mean = halves[0, 2 * lines :] / rows_all
        share = halves[:, lines : 2 * lines] / both_cols
        mean_square = spread_sum(share) * row_mean / (rows_all * columns_all)
    with jax.named_scope("update"):
        rate = step_size / jnp.maximum(1.0, jnp.sqrt(mean_square))
        col_factor = (lax.rsqrt(new_cols / row_mean) * rate).reshape(1, columns)
        row_factor = lax.rsqrt(new_rows)
        pair_weights = ordered(weights, other_weights)
        pair_new = [
            w - g * row_factor[x][:, None] * col_factor
            for x, (w, g) in enumerate(zip(pair_weights, gradient))
        ]
        new_weights = jnp.where(first, pair_new[0], pair_new[1])
        new_row_state = jnp.where(first, new_rows[0], new_rows[1])
        rounded = [w.astype(jnp.bfloat16) for w in pair_new]
    with jax.named_scope("gather_ring"):
        gathered = jnp.zeros((X_HALVES, n_z, rows, columns), jnp.bfloat16)

        def put(array, value, offset, x):
            start = (x, beside(offset), 0, 0)
            return lax.dynamic_update_slice(array, value[None, None], start)

        for x, r in enumerate(rounded):
            gathered = put(gathered, r, 0, x)
        held = [(r, r) for r in rounded]
        for hop in range(1, far):
            if hop == far - 1:
                last = [
                    lax.ppermute(held[x][x], ("dp", "row"), around_z(n_z, n_row, step))
                    for x, step in enumerate((2, -2))
                ]
            held = send_both(held)
            for x, (a, b) in enumerate(held):
                gathered = put(gathered, a, -hop, x)
                gathered = put(gathered, b, hop, x)
        for x, block_far in enumerate(last):
            gathered = put(gathered, block_far, far, x)
        compute_weights = gathered.reshape(n_dp * rows, columns)
    return (new_weights, compute_weights, new_row_state, new_cols.reshape(columns))


def solution(mesh):
    placed = (
        P(None, "dp", "row"),
        P(None, "dp", "col"),
        P(("row", "dp"), "col"),
        P(("row", "dp")),
        P("col"),
    )
    return jax.shard_map(
        shards,
        mesh=mesh,
        in_specs=placed,
        out_specs=(P(("row", "dp"), "col"), P("row", "col"), P(("row", "dp")), P("col")),
        check_vma=False,
    )
```

```python
import jax
import jax.numpy as jnp
from jax import lax
from jax.sharding import PartitionSpec as P

beta_two = 0.8
epsilon_one = 1e-30
step_size = 0.05

X_HALVES = 2
SEND_SCALE = 4.0
PARTS = 2


def around_z(n_z, n_row, hop):
    pairs = []
    for x in range(X_HALVES):
        for z in range(n_z):
            for row in range(n_row):
                there = (z + (hop if row % 2 == 0 else -hop)) % n_z
                pairs.append(((x * n_z + z) * n_row + row, (x * n_z + there) * n_row + row))
    return pairs


def across_x(n_z):
    return [(x * n_z + z, (1 - x) * n_z + z) for x in range(X_HALVES) for z in range(n_z)]


def shards(activations, cotangent, weights, row_state, col_state):
    f32, f16 = jnp.float32, jnp.float16
    lanes = 128
    n_dp = lax.axis_size("dp")
    n_row = lax.axis_size("row")
    n_z = n_dp // X_HALVES
    far = n_z // 2
    rows, columns = weights.shape
    rows_all = rows * n_dp * n_row
    columns_all = columns * lax.axis_size("col")
    place = lax.axis_index("dp")
    z = lax.rem(place, n_z)
    first = lax.div(place, n_z) == 0
    way = 1 - 2 * lax.rem(lax.axis_index("row"), 2)
    swap = across_x(n_z)
    ones = jnp.ones((lanes, lanes), f32)

    def spread_sum(array):
        return lax.dot_general(
            jnp.sum(array.reshape(-1, lanes), axis=0, keepdims=True),
            ones,
            (((1,), (0,)), ((), ())),
            precision=lax.Precision.HIGHEST,
            preferred_element_type=f32,
        )

    def ordered(own, other):
        return [jnp.where(first, own, other), jnp.where(first, other, own)]

    def beside(offset):
        return lax.rem(z + way * offset + n_z, n_z)

    def block(array, offset):
        return lax.dynamic_index_in_dim(array, beside(offset), 1, keepdims=False)

    def send_both(pairs, hop=1):
        both = ("dp", "row")
        up, down = around_z(n_z, n_row, hop), around_z(n_z, n_row, -hop)
        return [(lax.ppermute(a, both, up), lax.ppermute(b, both, down)) for a, b in pairs]

    with jax.named_scope("partner_weights"):
        other_weights = lax.ppermute(weights, "dp", swap)

    with jax.named_scope("gradient"):
        width = columns // PARTS
        sums = []
        for part in range(PARTS):
            product = lax.dot_general(
                activations,
                lax.slice_in_dim(cotangent, part * width, (part + 1) * width, axis=2),
                (((0, 1), (0, 1)), ((), ())),
                preferred_element_type=f32,
            )
            sums.append((product * SEND_SCALE).astype(f16).reshape(X_HALVES, n_z, rows, width))

    with jax.named_scope("reduce_ring"):
        leap = [
            lax.ppermute(block(s, far), ("dp", "row"), around_z(n_z, n_row, hop))
            for s, hop in zip(sums, (2, -2))
        ]
        held = send_both([(block(s, far - 1), block(s, 1 - far)) for s in sums])
        for hop in range(far - 2, 0, -1):
            sent = []
            for p, (s, (a, b)) in enumerate(zip(sums, held)):
                mine_up = block(s, hop).astype(f32) + a.astype(f32)
                mine_down = block(s, -hop).astype(f32) + b.astype(f32)
                if hop == far - 2 and p == 0:
                    mine_up = mine_up + leap[0].astype(f32)
                if hop == far - 2 and p == 1:
                    mine_down = mine_down + leap[1].astype(f32)
                sent.append((mine_up.astype(f16), mine_down.astype(f16)))
            held = send_both(sent)
        mine = [
            (block(s, 0).astype(f32) + a.astype(f32) + b.astype(f32)).astype(f16)
            for s, (a, b) in zip(sums, held)
        ]
    with jax.named_scope("reduce_pair"):
        theirs = [lax.ppermute(m, "dp", swap) for m in mine]
        both = jnp.concatenate(
            [
                (m.astype(f32) + t.astype(f32)) * (1.0 / SEND_SCALE)
                for m, t in zip(mine, theirs)
            ],
            axis=2,
        )
        gradient = [both[x] for x in range(X_HALVES)]
    with jax.named_scope("row_statistics"):
        local_rows = jnp.stack([jnp.sum(g * g, axis=1) for g in gradient])
        corner = [
            (2 * i + c, 2 * j + 1 - c) for i, j in across_x(n_z) for c in range(2)
        ]
        lines = columns // lanes
        tail = (0, max(rows, lanes) - rows)
        mail = [
            jnp.pad(local_rows, ((0, 0), tail)),
            jnp.pad(row_state[None], ((0, 0), tail)),
            jnp.pad(col_state.reshape(lines, lanes), ((0, 0), (0, max(rows, lanes) - lanes))),
        ]
        got = lax.ppermute(jnp.concatenate(mail), ("dp", "col"), corner)
        got_rows, got_state = got[:X_HALVES, :rows], got[X_HALVES, :rows]
        got_cols = got[X_HALVES + 1 :, :lanes]
        row_total = local_rows + got_rows
        pair_state = jnp.stack(ordered(row_state, got_state))
        new_rows = beta_two * pair_state + (1.0 - beta_two) * (
            row_total / columns_all + epsilon_one
        )
    with jax.named_scope("column_statistics"):
        inverse = 1.0 / new_rows
        local_cols = sum(jnp.sum(g * g, axis=0) for g in gradient)
        weighed_cols = sum(
            jnp.sum(g * g * inverse[x][:, None], axis=0) for x, g in enumerate(gradient)
        )
        pad = -(X_HALVES * rows) % lanes
        state_sum = spread_sum(jnp.pad(new_rows.reshape(-1), (0, pad)))
        vector = jnp.concatenate(
            [local_cols.reshape(-1, lanes), weighed_cols.reshape(-1, lanes), state_sum]
        )

        def spread(v, axis, size, groups=None):
            copies = jnp.broadcast_to(v[None], (size,) + v.shape)
            return lax.all_to_all(copies, axis, 0, 0, axis_index_groups=groups)

        z_groups = [[x * n_z + i for i in range(n_z)] for x in range(X_HALVES)]
        vector = jnp.sum(spread(vector, "dp", n_z, z_groups), axis=0)
        n_col = lax.axis_size("col")
        halves = spread(vector, ("row", "col"), n_row * n_col)
        halves = jnp.sum(halves.reshape(n_row, n_col, *vector.shape), axis=0)
        left = lax.axis_index("col") == 0
        own_cols = col_state.reshape(lines, lanes)
        states = jnp.stack(
            [jnp.where(left, own_cols, got_cols), jnp.where(left, got_cols, own_cols)]
        )
        both_cols = beta_two * states + (1.0 - beta_two) * (
            halves[:, :lines] / rows_all + epsilon_one
        )
        new_cols = jnp.where(left, both_cols[0], both_cols[1])
        row_mean = halves[0, 2 * lines :] / rows_all
        share = halves[:, lines : 2 * lines] / both_cols
        mean_square = spread_sum(share) * row_mean / (rows_all * columns_all)
    with jax.named_scope("update"):
        rate = step_size / jnp.maximum(1.0, jnp.sqrt(mean_square))
        col_factor = (lax.rsqrt(new_cols / row_mean) * rate).reshape(1, columns)
        row_factor = lax.rsqrt(new_rows)
        pair_weights = ordered(weights, other_weights)
        pair_new = [
            w - g * row_factor[x][:, None] * col_factor
            for x, (w, g) in enumerate(zip(pair_weights, gradient))
        ]
        new_weights = jnp.where(first, pair_new[0], pair_new[1])
        new_row_state = jnp.where(first, new_rows[0], new_rows[1])
        rounded = [w.astype(jnp.bfloat16) for w in pair_new]
    with jax.named_scope("gather_ring"):
        gathered = jnp.zeros((X_HALVES, n_z, rows, columns), jnp.bfloat16)

        def put(array, value, offset, x):
            start = (x, beside(offset), 0, 0)
            return lax.dynamic_update_slice(array, value[None, None], start)

        for x, r in enumerate(rounded):
            gathered = put(gathered, r, 0, x)
        held = [(r, r) for r in rounded]
        for hop in range(1, far):
            held = send_both(held)
            for x, (a, b) in enumerate(held):
                gathered = put(gathered, a, -hop, x)
                gathered = put(gathered, b, hop, x)
        for x, step in enumerate((1, -1)):
            found = lax.ppermute(held[x][x], ("dp", "row"), around_z(n_z, n_row, step))
            gathered = put(gathered, found, far, x)
        compute_weights = gathered.reshape(n_dp * rows, columns)
    return (new_weights, compute_weights, new_row_state, new_cols.reshape(columns))


def solution(mesh):
    placed = (
        P(None, "dp", "row"),
        P(None, "dp", "col"),
        P(("row", "dp"), "col"),
        P(("row", "dp")),
        P("col"),
    )
    return jax.shard_map(
        shards,
        mesh=mesh,
        in_specs=placed,
        out_specs=(P(("row", "dp"), "col"), P("row", "col"), P(("row", "dp")), P("col")),
        check_vma=False,
    )
```
